512 devices in a mesh: seq: 32 (over y, x), tensor: 16 (over z, core).
Axes of the slice: x: 4, y: 8, z: 8, core: 2. Of those that a mesh axis runs over, the one named last changes fastest.
Arguments:
- hidden: bfloat16 [2048, 28672], P('seq', 'tensor'), may hold values from -6 to 6
- down_weight: bfloat16 [28672, 8192], P('tensor', 'seq'), may hold values from -0.03125 to 0.03125
- delta_blocks: bfloat16 [32, 4096, 4096], P('seq', 'tensor'), may hold values from -0.08984375 to 0.08984375
- block_rows: int32 [32, 16, 256], replicated, may hold values from -1 to 27, as said below
- block_cols: int32 [32, 16, 256], replicated, may hold values from -1 to 127, as said below
- tenant_ids: int32 [2048], replicated, may hold values from 0 to 31, as said below
- tenant_lists: int32 [32, 128], replicated, may hold values from -1 to 2047, as said below
Outputs:
- mixed: bfloat16 [2048, 8192], P('tensor', 'seq')
The draws below stay inside these ranges and needn't reach their ends.
Inputs may be any that keep to these rules, and one draw needn't show every extreme that they name: `tenant_ids`: every variant names at least one and at most 128 tokens, and some variant names exactly 128. `tenant_lists`: row k lists, in ascending order, exactly the tokens whose tenant_ids entry is k, then -1 in the remaining slots. `block_rows`: slots g * 8 to (g + 1) * 8 - 1 of a list hold blocks whose column lies in g * 4 to (g + 1) * 4 - 1; live slots of one group come first, name distinct blocks, and in each list some group is full. Empty slots hold -1 here and in block_cols. `block_cols`: -1 marks an empty slot, exactly where block_rows holds -1.
All inputs are finite; a program needn't handle non-finite values.
Results may differ from the reference program's by a relative error of at most 0.0075.
Values may be sent and summed in bfloat16 or wider, within the bound.
No kernel may reach another device: no remote copies, remote signals or barrier semaphores. Data moves between devices by JAX's collectives and lax.ppermute only.
A program may use at most 128 MiB of HBM per device.

```python
import jax
import jax.numpy as jnp
from jax import lax

D = 8192
FF = 28672
BLK = 64
VARIANTS = 32
TOKENS = 2048
SHARDS = 16
RB = 28
CB = 4
BCAP = 8
NB = 256
BLOCKS = 4096
TCAP = 128


def tenant_layout(key):
    key = jax.random.fold_in(key, 11)
    first, second, third, fourth = jax.random.split(key, 4)
    slots = VARIANTS * TCAP
    owner = jnp.arange(slots, dtype=jnp.int32) // TCAP
    leading = jnp.arange(slots, dtype=jnp.int32) % TCAP == 0
    favour = jax.random.randint(first, (VARIANTS,), 0, 4)
    busiest = jax.random.randint(second, (), 0, VARIANTS)
    score = jax.random.randint(third, (slots,), 0, 1 << 12) + favour[owner] * (1 << 11)
    score = jnp.where((owner == busiest) | leading, 1 << 14, score)
    score = score * slots + jnp.arange(slots, dtype=jnp.int32)
    chosen = jnp.argsort(-score)[:TOKENS]
    picked = owner[chosen]
    mixing = jnp.argsort(jax.random.randint(fourth, (TOKENS,), 0, 1 << 16) * TOKENS + jnp.arange(TOKENS, dtype=jnp.int32))
    ids = jnp.zeros((TOKENS,), jnp.int32).at[mixing].set(picked)
    order = jnp.argsort(ids * TOKENS + jnp.arange(TOKENS, dtype=jnp.int32)).astype(jnp.int32)
    counts = jnp.sum((ids[None, :] == jnp.arange(VARIANTS, dtype=jnp.int32)[:, None]).astype(jnp.int32), axis=1)
    starts = jnp.cumsum(counts) - counts
    places = starts[:, None] + jnp.arange(TCAP, dtype=jnp.int32)[None, :]
    lists = jnp.where(jnp.arange(TCAP, dtype=jnp.int32)[None, :] < counts[:, None], order[jnp.clip(places, 0, TOKENS - 1)], -1)
    return (ids.astype(jnp.int32), lists.astype(jnp.int32))


def block_layout(key):
    key = jax.random.fold_in(key, 23)
    first, second, third = jax.random.split(key, 3)
    groups = NB // BCAP
    candidates = RB * CB
    scores = jax.random.randint(first, (VARIANTS, SHARDS, groups, candidates), 0, 1 << 18) * candidates + jnp.arange(candidates, dtype=jnp.int32)
    order = jnp.argsort(scores, axis=-1)[..., :BCAP].astype(jnp.int32)
    counts = jax.random.randint(second, (VARIANTS, SHARDS, groups), (BCAP + 1) // 2, BCAP + 1)
    fullest = jax.random.randint(third, (VARIANTS, SHARDS, 1), 0, groups)
    counts = jnp.where(jnp.arange(groups, dtype=jnp.int32)[None, None, :] == fullest, BCAP, counts)
    live = jnp.arange(BCAP, dtype=jnp.int32)[None, None, None, :] < counts[..., None]
    rows = jnp.where(live, order // CB, -1)
    cols = jnp.where(live, order % CB + (jnp.arange(groups, dtype=jnp.int32) * CB)[None, None, :, None], -1)
    return (rows.reshape(VARIANTS, SHARDS, NB).astype(jnp.int32), cols.reshape(VARIANTS, SHARDS, NB).astype(jnp.int32))


def draw_tenant_ids(key, part):
    return tenant_layout(key)[0]


def draw_tenant_lists(key, part):
    return tenant_layout(key)[1]


def draw_block_rows(key, part):
    return block_layout(key)[0]


def draw_block_cols(key, part):
    return block_layout(key)[1]


def steps_of(rng, dims, cuts, least, top_value):
    factor_of, own = 1.0, jax.random.fold_in(rng, 6)
    for axis_at, shards_of in cuts:
        draws = jnp.exp(jax.random.uniform(jax.random.fold_in(own, axis_at), (shards_of,), jnp.float32, least / len(cuts), top_value / len(cuts)))
        factor_of = factor_of * jnp.repeat(draws, dims[axis_at] // shards_of).reshape([-1 if axis == axis_at else 1 for axis in range(len(dims))])
    return factor_of


def normal_values(stream_key, shape, scale, most, cuts=(), kind=jnp.bfloat16):
    entries = scale * jax.random.normal(stream_key, shape, jnp.float32)
    if cuts:
        entries = entries * steps_of(stream_key, shape, cuts, -0.22, 0.18)
    return jnp.clip(entries, -most, most).astype(kind)


def setup_inputs(seed: int = 0) -> dict:
    splits = jax.random.split(jax.random.key(seed), 8)
    return {
        "hidden": normal_values(splits[0], (TOKENS, FF), 1.0, 6.0, ((0, 32), (1, 16))),
        "down_weight": normal_values(splits[1], (FF, D), FF ** -0.5, 0.03125, ((0, 16), (1, 32))),
        "delta_blocks": normal_values(splits[2], (VARIANTS, BLOCKS, BLK * BLK), 0.015, 0.08984375, ((0, 32), (1, 16))),
        "block_rows": draw_block_rows(jax.random.fold_in(splits[7], 71), 0),
        "block_cols": draw_block_cols(jax.random.fold_in(splits[7], 71), 0),
        "tenant_ids": draw_tenant_ids(jax.random.fold_in(splits[7], 71), 0),
        "tenant_lists": draw_tenant_lists(jax.random.fold_in(splits[7], 71), 0),
    }


def one_variant(hidden, chosen, blocks, rows, cols):
    capacity = chosen.shape[0]
    safe = jnp.clip(chosen, 0, hidden.shape[0] - 1).astype(jnp.int32)
    picked = jnp.where((chosen >= 0)[:, None], hidden[safe], jnp.zeros((capacity, hidden.shape[1]), hidden.dtype))
    grid = picked.reshape(capacity, SHARDS * RB, BLK)
    global_rows = (jnp.clip(rows, 0, RB - 1) + (jnp.arange(SHARDS, dtype=jnp.int32) * RB)[:, None]).astype(jnp.int32)
    pieces = grid[:, global_rows]
    matrices = blocks.reshape(SHARDS, NB, BLK, BLK)
    products = jnp.einsum("tsnb,snbc->tsnc", pieces.astype(jnp.float32), matrices.astype(jnp.float32), precision=lax.Precision.HIGHEST)
    groups = NB // BCAP
    grouped = products.reshape(capacity, SHARDS, groups, BCAP, BLK)
    offsets = cols.reshape(SHARDS, groups, BCAP) - (jnp.arange(groups, dtype=jnp.int32) * CB)[None, :, None]
    selector = (offsets[..., None] == jnp.arange(CB, dtype=jnp.int32)).astype(jnp.float32)
    placed = jnp.einsum("tsgbx,sgbc->tgcx", grouped, selector, precision=lax.Precision.HIGHEST)
    return placed.reshape(capacity, groups * CB * BLK)


def reference(hidden, down_weight, delta_blocks, block_rows, block_cols, tenant_ids, tenant_lists):
    base = jnp.dot(hidden, down_weight, preferred_element_type=jnp.float32)
    variant_count, capacity = tenant_lists.shape

    def step(args):
        chosen, blocks, rows, cols = args
        return one_variant(hidden, chosen, blocks, rows, cols)

    deltas = lax.map(step, (tenant_lists, delta_blocks, block_rows, block_cols))
    match = tenant_ids[:, None] == jnp.arange(variant_count, dtype=jnp.int32)[None, :]
    running = jnp.cumsum(match.astype(jnp.int32), axis=0) - 1
    rank = jnp.sum(jnp.where(match, running, 0), axis=1).astype(jnp.int32)
    flat = deltas.reshape(variant_count * capacity, deltas.shape[2])
    where_row = (tenant_ids * capacity + rank).astype(jnp.int32)
    return (base + flat[where_row]).astype(jnp.bfloat16)
```

```python
import jax
import jax.numpy as jnp
from jax import lax
from jax.experimental import pallas as pl
from jax.experimental.pallas import tpu as pltpu
from jax.sharding import Mesh, PartitionSpec as P

BLK = 64
LANES = 128
SEQ = ("y", "x")
TENSOR = ("z", "core")
CORE_SWAP = [(0, 1), (1, 0)]


def delta_kernel(rows, cols, own_rows, other_rows, own_blocks, other_blocks, out, table):
    group = pl.program_id(0)
    per_group, half_rows, _ = own_blocks.shape
    tiles = own_rows.shape[1] // LANES
    low = lax.broadcasted_iota(jnp.int32, (1, LANES), 1) < BLK
    low_f = low.astype(jnp.float32).astype(jnp.bfloat16)
    high_f = (~low).astype(jnp.float32).astype(jnp.bfloat16)

    @pl.when(group == 0)
    def _():
        source = lax.broadcasted_iota(jnp.int32, (LANES, 2 * LANES), 0)
        place = lax.broadcasted_iota(jnp.int32, (LANES, 2 * LANES), 1)
        copy, lane = place // LANES, place % LANES
        half = (lane // BLK) ^ copy
        inner = lane % BLK
        wanted = half * BLK + (inner % (BLK // 2)) * 2 + inner // (BLK // 2)
        order = (source == wanted).astype(jnp.float32).astype(jnp.bfloat16)
        for side, ref in enumerate((own_rows, other_rows)):
            for tile in range(tiles):
                both = jnp.dot(
                    ref[:, tile * LANES : (tile + 1) * LANES], order, preferred_element_type=jnp.float32
                ).astype(jnp.bfloat16)
                table[(side * 2) * tiles + tile] = both[:, :LANES]
                table[(side * 2 + 1) * tiles + tile] = both[:, LANES:]

    lane_col = lax.broadcasted_iota(jnp.int32, (1, LANES), 1) // BLK
    pieces, weights = [], []
    for side, blocks in enumerate((own_blocks, other_blocks)):
        for pair in range(per_group // 2):
            picked = []
            for position in range(2):
                n = pair * 2 + position
                slot = group * per_group + n
                row = jnp.maximum(rows[side, slot], 0)
                swapped = (row & 1) ^ position
                picked.append(table[(side * 2 + swapped) * tiles + row // 2])
                column = cols[side, slot]
                column = jnp.where(column >= 0, column & 3, -1)
                block = blocks[n]
                turned = pltpu.roll(block.astype(jnp.float32), BLK, 1).astype(jnp.bfloat16)
                evens = block * low_f + turned * high_f
                odds = turned * low_f + block * high_f
                first = (lane_col == column).astype(jnp.float32).astype(jnp.bfloat16)
                second = (lane_col + 2 == column).astype(jnp.float32).astype(jnp.bfloat16)
                weights.append(jnp.concatenate([evens * first, evens * second], axis=1))
                weights.append(jnp.concatenate([odds * first, odds * second], axis=1))
            pieces.append(picked[0] * low_f + picked[1] * high_f)
    left = jnp.concatenate(pieces, axis=1)
    right = jnp.concatenate(weights, axis=0)
    out[0] = jnp.dot(left, right, preferred_element_type=jnp.float32).astype(out.dtype)


def delta_products(rows, cols, own_rows, other_rows, own_blocks, other_blocks, groups, width):
    count, ff = own_rows.shape
    slots, half_rows, lanes = own_blocks.shape
    per_group = slots // groups
    fixed = pl.BlockSpec((count, ff), lambda g, *_: (0, 0))
    blocks = pl.BlockSpec((per_group, half_rows, lanes), lambda g, *_: (g, 0, 0))
    return pl.pallas_call(
        delta_kernel,
        grid_spec=pltpu.PrefetchScalarGridSpec(
            num_scalar_prefetch=2,
            grid=(groups,),
            in_specs=[fixed, fixed, blocks, blocks],
            out_specs=pl.BlockSpec((1, count, width), lambda g, *_: (g, 0, 0)),
            scratch_shapes=[pltpu.VMEM((4 * ff // LANES, count, LANES), jnp.bfloat16)],
        ),
        out_shape=jax.ShapeDtypeStruct((groups, count, width), jnp.bfloat16),
        compiler_params=pltpu.CompilerParams(vmem_limit_bytes=24 * 2**20),
    )(rows, cols, own_rows, other_rows, own_blocks, other_blocks)


def place_kernel(core, tokens, rows, base, out):
    tile = pl.program_id(0) * 2 + pl.program_id(1)
    count = base.shape[0]
    token = lax.broadcasted_iota(jnp.int32, (count, 1), 0) + tile * count
    hot = (tokens[...] == token).astype(jnp.float32).astype(jnp.bfloat16)
    moved = jnp.dot(hot, rows[...], preferred_element_type=jnp.float32)
    out[0, 0] = (moved + base[...]).astype(out.dtype)


def place_rows(core, tokens, rows, base, planes):
    total, width = base.shape
    count = total // planes // 2
    return pl.pallas_call(
        place_kernel,
        grid_spec=pltpu.PrefetchScalarGridSpec(
            num_scalar_prefetch=1,
            grid=(planes, 2),
            in_specs=[
                pl.BlockSpec((1, tokens.shape[1]), lambda z, c, core: (0, 0)),
                pl.BlockSpec(rows.shape, lambda z, c, core: (0, 0)),
                pl.BlockSpec((count, width), lambda z, c, core: (z * 2 + c, 0)),
            ],
            out_specs=pl.BlockSpec((1, 1, count, width), lambda z, c, core: (c ^ core[0], z, 0, 0)),
        ),
        out_shape=jax.ShapeDtypeStruct((2, planes, count, width), jnp.bfloat16),
        compiler_params=pltpu.CompilerParams(vmem_limit_bytes=24 * 2**20),
    )(core, tokens, rows, base)


def per_device(hidden, down_weight, delta_blocks, block_rows, block_cols, tenant_ids, tenant_lists):
    core = lax.axis_index("core")
    seq_index = lax.axis_index(SEQ)
    tensor_index = lax.axis_index(TENSOR)
    seq_count = lax.axis_size(SEQ)
    planes = lax.axis_size("z")
    variants, capacity = tenant_lists.shape
    half = capacity // 2
    ff_local, width = down_weight.shape
    slots = delta_blocks.shape[1]

    own_blocks = delta_blocks[0].reshape(slots, BLK // 2, 2 * BLK)
    other_blocks = lax.ppermute(own_blocks, "core", CORE_SWAP)
    pair = jnp.stack([tensor_index, tensor_index ^ 1])
    rows = lax.dynamic_index_in_dim(block_rows, seq_index, 0, False)[pair]
    cols = lax.dynamic_index_in_dim(block_cols, seq_index, 0, False)[pair]

    gathered = lax.all_gather(hidden, SEQ, axis=0, tiled=True)
    tokens = gathered.shape[0]
    own_list = lax.dynamic_index_in_dim(tenant_lists, seq_index, 0, False).reshape(2, half)
    ordered = jnp.stack([own_list[core], own_list[1 - core]]).reshape(capacity)
    hot = (ordered[:, None] == jnp.arange(tokens, dtype=jnp.int32)[None, :]).astype(jnp.bfloat16)
    picked = jnp.dot(hot, gathered, preferred_element_type=jnp.float32).astype(jnp.bfloat16)
    other_picked = lax.ppermute(picked[half:], "core", CORE_SWAP)
    delta = delta_products(rows, cols, picked[:half], other_picked, own_blocks, other_blocks, seq_count, width)
    received = lax.all_to_all(delta, SEQ, split_axis=0, concat_axis=0, tiled=True)
    base = jnp.dot(gathered, down_weight, preferred_element_type=jnp.float32)
    lists = tenant_lists.reshape(variants, 2, half)
    held = lax.dynamic_index_in_dim(lists, core, 1, False).reshape(1, variants * half)
    partial = place_rows(core.reshape(1).astype(jnp.int32), held, received.reshape(variants * half, width), base, planes)
    swapped = lax.ppermute(partial[1], "core", CORE_SWAP)
    summed = (partial[0].astype(jnp.float32) + swapped.astype(jnp.float32)).astype(jnp.bfloat16)
    parts = lax.all_to_all(summed, "z", split_axis=0, concat_axis=0, tiled=True)
    return jnp.sum(parts.astype(jnp.float32), axis=0).astype(jnp.bfloat16)


def solution(mesh):
    fine = Mesh(mesh.devices.reshape(8, 4, 8, 2), ("y", "x", "z", "core"))
    return jax.shard_map(
        per_device,
        mesh=fine,
        in_specs=(
            P(SEQ, TENSOR),
            P(TENSOR, SEQ),
            P(SEQ, TENSOR, None),
            P(),
            P(),
            P(),
            P(),
        ),
        out_specs=P(TENSOR, SEQ),
        check_vma=False,
    )
```

```python
import jax
import jax.numpy as jnp
from jax import lax
from jax.experimental import pallas as pl
from jax.experimental.pallas import tpu as pltpu
from jax.sharding import Mesh, PartitionSpec as P

BLK = 64
LANES = 128
SEQ = ("y", "x")
TENSOR = ("z", "core")
CHIPS = ("x", "core")
CORE_SWAP = [(0, 1), (1, 0)]
STEP_GROUPS = 2
SPREAD_GROUPS = 4


def as_bf16(mask):
    return mask.astype(jnp.float32).astype(jnp.bfloat16)


def spread_kernel(core, own, other, lists, tokens, out, hot):
    low = lax.broadcasted_iota(jnp.int32, (1, LANES), 1) < BLK
    low_f, high_f = as_bf16(low), as_bf16(~low)
    hot[...] = as_bf16(lists[...] == tokens[...])

    def spread(blocks):
        for n in range(blocks.shape[0]):
            block = blocks[n]
            turned = pltpu.roll(block.astype(jnp.float32), BLK, 1).astype(jnp.bfloat16)
            out[0, n, : BLK // 2] = block * low_f + turned * high_f
            out[0, n, BLK // 2 :] = turned * low_f + block * high_f

    pl.when(pl.program_id(0) == 0)(lambda: spread(own))
    pl.when(pl.program_id(0) == 1)(lambda: spread(other))


def spread_blocks(core, own, other, lists, tokens, groups):
    slots, half_rows, lanes = own.shape
    steps = groups // SPREAD_GROUPS
    count = slots // steps
    picks = lists.shape[0]
    return pl.pallas_call(
        spread_kernel,
        grid_spec=pltpu.PrefetchScalarGridSpec(
            num_scalar_prefetch=1,
            grid=(2, steps),
            in_specs=[
                pl.BlockSpec((count, half_rows, lanes), lambda s, g, *_: (g * (1 - s) + (steps - 1) * s, 0, 0)),
                pl.BlockSpec((count, half_rows, lanes), lambda s, g, *_: (g * s, 0, 0)),
                pl.BlockSpec((picks // steps, 1), lambda s, g, *_: (g, 0)),
                pl.BlockSpec(tokens.shape, lambda s, g, *_: (0, 0)),
            ],
            out_specs=[
                pl.BlockSpec((1, count, BLK, LANES), lambda s, g, core: (s ^ core[0], g, 0, 0)),
                pl.BlockSpec((picks // steps, tokens.shape[1]), lambda s, g, *_: (g, 0)),
            ],
        ),
        out_shape=[
            jax.ShapeDtypeStruct((2, slots, BLK, LANES), jnp.bfloat16),
            jax.ShapeDtypeStruct((picks, tokens.shape[1]), jnp.bfloat16),
        ],
        compiler_params=pltpu.CompilerParams(vmem_limit_bytes=16 * 2**20),
        cost_estimate=pl.CostEstimate(flops=0, bytes_accessed=40_000_000, transcendentals=0),
    )(core, own, other, lists, tokens)


def delta_kernel(rows, cols, *refs):
    *sent, weights, out, table = refs
    step = pl.program_id(0)
    per_group = weights.shape[1] // STEP_GROUPS
    tiles = sum(ref.shape[2] for ref in sent) // LANES
    lane_col = lax.broadcasted_iota(jnp.int32, (1, LANES), 1) // BLK
    low_f, high_f = as_bf16(lane_col == 0), as_bf16(lane_col == 1)

    @pl.when(step == 0)
    def _():
        source = lax.broadcasted_iota(jnp.int32, (LANES, 2 * LANES), 0)
        place = lax.broadcasted_iota(jnp.int32, (LANES, 2 * LANES), 1)
        copy, lane = place // LANES, place % LANES
        half = (lane // BLK) ^ copy
        inner = lane % BLK
        wanted = half * BLK + (inner % (BLK // 2)) * 2 + inner // (BLK // 2)
        order = as_bf16(source == wanted)
        for side in range(2):
            tile = 0
            for ref in sent:
                for at in range(0, ref.shape[2], LANES):
                    mine = ref[side, :, at : at + LANES]
                    for x in range(1, ref.shape[0] // 2):
                        mine = mine + ref[2 * x + side, :, at : at + LANES]
                    both = jnp.dot(mine, order, preferred_element_type=jnp.float32).astype(jnp.bfloat16)
                    table[(side * 2) * tiles + tile] = both[:, :LANES]
                    table[(side * 2 + 1) * tiles + tile] = both[:, LANES:]
                    tile += 1

    for inner in range(STEP_GROUPS):
        total = None
        for side in range(2):
            pieces, spread = [], []
            for pair in range(per_group // 2):
                picked = []
                for position in range(2):
                    n = inner * per_group + pair * 2 + position
                    slot = step * STEP_GROUPS * per_group + n
                    row = jnp.maximum(rows[side, slot], 0)
                    swapped = (row & 1) ^ position
                    picked.append(table[(side * 2 + swapped) * tiles + row // 2])
                    column = cols[side, slot]
                    column = jnp.where(column >= 0, column & 3, -1)
                    block = weights[side, n]
                    spread.append(
                        jnp.concatenate(
                            [block * as_bf16(lane_col == column), block * as_bf16(lane_col + 2 == column)], axis=1
                        )
                    )
                pieces.append(picked[0] * low_f + picked[1] * high_f)
            product = jnp.dot(
                jnp.concatenate(pieces, axis=1), jnp.concatenate(spread, axis=0), preferred_element_type=jnp.float32
            )
            total = product if total is None else total + product
        out[inner] = total.astype(out.dtype)


def delta_products(rows, cols, sent, weights, groups, width):
    slots = weights.shape[1]
    per_step = slots // groups * STEP_GROUPS
    count = sent[0].shape[1]
    tiles = sum(a.shape[2] for a in sent) // LANES
    return pl.pallas_call(
        delta_kernel,
        grid_spec=pltpu.PrefetchScalarGridSpec(
            num_scalar_prefetch=2,
            grid=(groups // STEP_GROUPS,),
            in_specs=[pl.BlockSpec(a.shape, lambda g, *_: (0, 0, 0)) for a in sent]
            + [pl.BlockSpec((2, per_step, BLK, LANES), lambda g, *_: (0, g, 0, 0))],
            out_specs=pl.BlockSpec((STEP_GROUPS, count, width), lambda g, *_: (g, 0, 0)),
            scratch_shapes=[pltpu.VMEM((4 * tiles, count, LANES), jnp.bfloat16)],
        ),
        out_shape=jax.ShapeDtypeStruct((groups, count, width), jnp.bfloat16),
        compiler_params=pltpu.CompilerParams(vmem_limit_bytes=24 * 2**20),
        cost_estimate=pl.CostEstimate(flops=2 * 10**9, bytes_accessed=20_000_000, transcendentals=0),
    )(rows, cols, *sent, weights)


def base_kernel(tokens, weights, out):
    product = jnp.dot(tokens[...], weights[0], preferred_element_type=jnp.float32)
    out[:, 0, 0] = product.reshape(out.shape[0], out.shape[3], out.shape[4])


def base_products(tokens, weights, planes):
    count, depth = tokens.shape
    columns, _, width = weights.shape
    return pl.pallas_call(
        base_kernel,
        grid=(columns,),
        in_specs=[
            pl.BlockSpec((count, depth), lambda x: (0, 0)),
            pl.BlockSpec((1, depth, width), lambda x: (x, 0, 0)),
        ],
        out_specs=pl.BlockSpec((planes, 1, 1, count // planes, width), lambda x: (0, x // 2, x % 2, 0, 0)),
        out_shape=jax.ShapeDtypeStruct((planes, 2, columns // 2, count // planes, width), jnp.float32),
        compiler_params=pltpu.CompilerParams(vmem_limit_bytes=24 * 2**20),
        cost_estimate=pl.CostEstimate(flops=2 * 10**9, bytes_accessed=8_000_000, transcendentals=0),
    )(tokens, weights)


def place_kernel(core, tokens, rows, out):
    count = out.shape[2]
    token = lax.broadcasted_iota(jnp.int32, (2 * count, 1), 0) + pl.program_id(0) * 2 * count
    hot = as_bf16(tokens[...] == token)
    placed = jnp.dot(hot, rows[...], preferred_element_type=jnp.float32).astype(out.dtype)
    for c in range(2):
        out[c ^ core[0], 0] = placed[c * count : (c + 1) * count]


def place_rows(core, tokens, rows, planes, count):
    width = rows.shape[1]
    return pl.pallas_call(
        place_kernel,
        grid_spec=pltpu.PrefetchScalarGridSpec(
            num_scalar_prefetch=1,
            grid=(planes,),
            in_specs=[
                pl.BlockSpec((1, tokens.shape[1]), lambda z, *_: (0, 0)),
                pl.BlockSpec(rows.shape, lambda z, *_: (0, 0)),
            ],
            out_specs=pl.BlockSpec((2, 1, count, width), lambda z, *_: (0, z, 0, 0)),
        ),
        out_shape=jax.ShapeDtypeStruct((2, planes, count, width), jnp.bfloat16),
        compiler_params=pltpu.CompilerParams(vmem_limit_bytes=24 * 2**20),
        cost_estimate=pl.CostEstimate(flops=2 * 10**9, bytes_accessed=8_000_000, transcendentals=0),
    )(core, tokens, rows)


def core_sum(pair):
    swapped = lax.ppermute(pair[1], "core", CORE_SWAP)
    return (pair[0].astype(jnp.float32) + swapped.astype(jnp.float32)).astype(jnp.bfloat16)


def plane_sum(values):
    parts = lax.all_to_all(values, "z", split_axis=0, concat_axis=0, tiled=True)
    return jnp.sum(parts.astype(jnp.float32), axis=0)


def per_device(hidden, down_weight, delta_blocks, block_rows, block_cols, tenant_ids, tenant_lists):
    core, column, line = lax.axis_index("core"), lax.axis_index("x"), lax.axis_index("y")
    seq_index = lax.axis_index(SEQ)
    plane = lax.axis_index("z")
    seq_count, lines, columns, planes = (lax.axis_size(a) for a in (SEQ, "y", "x", "z"))
    variants, capacity = tenant_lists.shape
    half = capacity // 2
    own_tokens = hidden.shape[0]
    ff_local, width = down_weight.shape
    slots = delta_blocks.shape[1]
    core_ref = core.reshape(1).astype(jnp.int32)

    gathered = lax.all_gather(hidden, "y", axis=0, tiled=True)
    copies = jnp.broadcast_to(down_weight[None], (columns, ff_local, width))
    weights = lax.all_to_all(copies, "x", split_axis=0, concat_axis=0, tiled=True)

    own_blocks = delta_blocks[0].reshape(slots, BLK // 2, 2 * BLK)
    other_blocks = lax.ppermute(own_blocks, "core", CORE_SWAP)
    rows = lax.dynamic_index_in_dim(block_rows, seq_index, 0, False)
    rows = lax.dynamic_slice_in_dim(rows, plane * 2, 2, 0)
    cols = lax.dynamic_index_in_dim(block_cols, seq_index, 0, False)
    cols = lax.dynamic_slice_in_dim(cols, plane * 2, 2, 0)
    lists = lax.dynamic_index_in_dim(tenant_lists.reshape(lines, columns * capacity), line, 0, False)
    token = jnp.arange(lines * own_tokens, dtype=jnp.int32)
    token = ((token // own_tokens) * columns + column) * own_tokens + token % own_tokens
    spread, hot = spread_blocks(
        core_ref, own_blocks, other_blocks, lists[:, None], token[None, :], seq_count
    )

    picked = jnp.dot(hot, gathered, preferred_element_type=jnp.float32).astype(jnp.bfloat16)
    picked = picked.reshape(columns * 2, half, ff_local)
    sent = lax.all_to_all(picked, CHIPS, split_axis=0, concat_axis=0, tiled=True)
    delta = delta_products(rows, cols, [sent], spread, seq_count, width)
    received = lax.all_to_all(delta, SEQ, split_axis=0, concat_axis=0, tiled=True)

    base = base_products(gathered, weights, planes)
    base = lax.psum_scatter(
        base.reshape(planes * 2, columns // 2 * own_tokens, width), TENSOR, scatter_dimension=0, tiled=True
    )
    base = base.reshape(columns // 2, own_tokens, width)
    odd = column % 2
    blocks = []
    for flip in range(2):
        pairs = []
        for x in range(columns):
            for c in range(2):
                pairs.append((x * 2 + c, (2 * c + (x % 2 ^ flip)) * 2 + x // 2))
        mine = lax.dynamic_index_in_dim(base, odd ^ flip, 0, False)
        blocks.append(lax.ppermute(mine, CHIPS, pairs))
    base = jnp.where(odd == 0, jnp.concatenate(blocks, 0), jnp.concatenate(blocks[::-1], 0))

    held = lax.dynamic_index_in_dim(tenant_lists.reshape(variants, 2, half), core, 1, False)
    placed = place_rows(
        core_ref,
        held.reshape(1, variants * half),
        received.reshape(variants * half, width),
        planes,
        base.shape[0],
    )
    return (plane_sum(core_sum(placed)) + base).astype(jnp.bfloat16)


def solution(mesh):
    fine = Mesh(mesh.devices.reshape(8, 4, 8, 2), ("y", "x", "z", "core"))
    return jax.shard_map(
        per_device,
        mesh=fine,
        in_specs=(
            P(SEQ, TENSOR),
            P(TENSOR, SEQ),
            P(SEQ, TENSOR, None),
            P(),
            P(),
            P(),
            P(),
        ),
        out_specs=P(TENSOR, SEQ),
        check_vma=False,
    )
```

```python
import jax
import jax.numpy as jnp
from jax import lax
from jax.experimental import pallas as pl
from jax.experimental.pallas import tpu as pltpu
from jax.sharding import Mesh, PartitionSpec as P

BLK = 64
LANES = 128
SEQ = ("y", "x")
TENSOR = ("z", "core")
CHIPS = ("x", "core")
CORE_SWAP = [(0, 1), (1, 0)]
STEP_GROUPS = 4
SPREAD_GROUPS = 4


def as_bf16(mask):
    return mask.astype(jnp.float32).astype(jnp.bfloat16)


def spread_kernel(core, own, other, lists, tokens, out, hot):
    low = lax.broadcasted_iota(jnp.int32, (1, LANES), 1) < BLK
    low_f, high_f = as_bf16(low), as_bf16(~low)
    hot[...] = as_bf16(lists[...] == tokens[...])

    def spread(blocks):
        for n in range(blocks.shape[0]):
            block = blocks[n]
            turned = pltpu.roll(block.astype(jnp.float32), BLK, 1).astype(jnp.bfloat16)
            out[0, n, : BLK // 2] = block * low_f + turned * high_f
            out[0, n, BLK // 2 :] = turned * low_f + block * high_f

    pl.when(pl.program_id(0) == 0)(lambda: spread(own))
    pl.when(pl.program_id(0) == 1)(lambda: spread(other))


def spread_blocks(core, own, other, lists, tokens, groups):
    slots, half_rows, lanes = own.shape
    steps = groups // SPREAD_GROUPS
    count = slots // steps
    picks = lists.shape[0]
    return pl.pallas_call(
        spread_kernel,
        grid_spec=pltpu.PrefetchScalarGridSpec(
            num_scalar_prefetch=1,
            grid=(2, steps),
            in_specs=[
                pl.BlockSpec((count, half_rows, lanes), lambda s, g, *_: (g * (1 - s) + (steps - 1) * s, 0, 0)),
                pl.BlockSpec((count, half_rows, lanes), lambda s, g, *_: (g * s, 0, 0)),
                pl.BlockSpec((picks // steps, 1), lambda s, g, *_: (g, 0)),
                pl.BlockSpec(tokens.shape, lambda s, g, *_: (0, 0)),
            ],
            out_specs=[
                pl.BlockSpec((1, count, BLK, LANES), lambda s, g, core: (s ^ core[0], g, 0, 0)),
                pl.BlockSpec((picks // steps, tokens.shape[1]), lambda s, g, *_: (g, 0)),
            ],
        ),
        out_shape=[
            jax.ShapeDtypeStruct((2, slots, BLK, LANES), jnp.bfloat16),
            jax.ShapeDtypeStruct((picks, tokens.shape[1]), jnp.bfloat16),
        ],
        compiler_params=pltpu.CompilerParams(vmem_limit_bytes=56 * 2**20),
        cost_estimate=pl.CostEstimate(flops=0, bytes_accessed=40_000_000, transcendentals=0),
    )(core, own, other, lists, tokens)


def delta_kernel(rows, cols, *refs):
    *sent, stored, out, table, weights, arrived = refs
    step, steps = pl.program_id(0), arrived.shape[0]
    count = stored.shape[1] // steps
    per_group = count // STEP_GROUPS

    def fetch(at):
        slots = pl.ds(pl.multiple_of(at * count, count), count)
        return pltpu.make_async_copy(stored.at[:, slots], weights.at[:, slots], arrived.at[at])

    @pl.when(step == 0)
    def _():
        lax.fori_loop(0, steps, lambda at, _: fetch(at).start(), None)

    tiles = sum(ref.shape[2] for ref in sent) // LANES
    lane_col = lax.broadcasted_iota(jnp.int32, (1, LANES), 1) // BLK
    low_f, high_f = as_bf16(lane_col == 0), as_bf16(lane_col == 1)

    @pl.when(step == 0)
    def _():
        source = lax.broadcasted_iota(jnp.int32, (LANES, 2 * LANES), 0)
        place = lax.broadcasted_iota(jnp.int32, (LANES, 2 * LANES), 1)
        copy, lane = place // LANES, place % LANES
        half = (lane // BLK) ^ copy
        inner = lane % BLK
        wanted = half * BLK + (inner % (BLK // 2)) * 2 + inner // (BLK // 2)
        order = as_bf16(source == wanted)
        for side in range(2):
            tile = 0
            for ref in sent:
                for at in range(0, ref.shape[2], LANES):
                    mine = ref[side, :, at : at + LANES]
                    for x in range(1, ref.shape[0] // 2):
                        mine = mine + ref[2 * x + side, :, at : at + LANES]
                    both = jnp.dot(mine, order, preferred_element_type=jnp.float32).astype(jnp.bfloat16)
                    table[(side * 2) * tiles + tile] = both[:, :LANES]
                    table[(side * 2 + 1) * tiles + tile] = both[:, LANES:]
                    tile += 1

    fetch(step).wait()
    for inner in range(STEP_GROUPS):
        total = None
        for side in range(2):
            pieces, spread = [], []
            for pair in range(per_group // 2):
                picked = []
                for position in range(2):
                    n = inner * per_group + pair * 2 + position
                    slot = step * STEP_GROUPS * per_group + n
                    row = jnp.maximum(rows[side, slot], 0)
                    swapped = (row & 1) ^ position
                    picked.append(table[(side * 2 + swapped) * tiles + row // 2])
                    column = cols[side, slot]
                    column = jnp.where(column >= 0, column & 3, -1)
                    block = weights[side, step * count + n]
                    spread.append(
                        jnp.concatenate(
                            [block * as_bf16(lane_col == column), block * as_bf16(lane_col + 2 == column)], axis=1
                        )
                    )
                pieces.append(picked[0] * low_f + picked[1] * high_f)
            product = jnp.dot(
                jnp.concatenate(pieces, axis=1), jnp.concatenate(spread, axis=0), preferred_element_type=jnp.float32
            )
            total = product if total is None else total + product
        out[inner] = total.astype(out.dtype)


def delta_products(rows, cols, sent, weights, groups, width):
    count = sent[0].shape[1]
    tiles = sum(a.shape[2] for a in sent) // LANES
    return pl.pallas_call(
        delta_kernel,
        grid_spec=pltpu.PrefetchScalarGridSpec(
            num_scalar_prefetch=2,
            grid=(groups // STEP_GROUPS,),
            in_specs=[pl.BlockSpec(a.shape, lambda g, *_: (0, 0, 0)) for a in sent]
            + [pl.BlockSpec(memory_space=pl.ANY)],
            out_specs=pl.BlockSpec((STEP_GROUPS, count, width), lambda g, *_: (g, 0, 0)),
            scratch_shapes=[
                pltpu.VMEM((4 * tiles, count, LANES), jnp.bfloat16),
                pltpu.VMEM(weights.shape, jnp.bfloat16),
                pltpu.SemaphoreType.DMA((groups // STEP_GROUPS,)),
            ],
        ),
        out_shape=jax.ShapeDtypeStruct((groups, count, width), jnp.bfloat16),
        compiler_params=pltpu.CompilerParams(vmem_limit_bytes=48 * 2**20),
        cost_estimate=pl.CostEstimate(flops=2 * 10**9, bytes_accessed=20_000_000, transcendentals=0),
    )(rows, cols, *sent, weights)


def pick_kernel(hot, *refs):
    *parts, out = refs
    at = 0
    for part in parts:
        depth = part.shape[1]
        picked = jnp.dot(hot[...], part[...], preferred_element_type=jnp.float32)
        out[:, at : at + depth] = picked.astype(out.dtype)
        at += depth


def pick_rows(hot, parts):
    picks, count = hot.shape
    depth = sum(a.shape[1] for a in parts)
    return pl.pallas_call(
        pick_kernel,
        grid=(2,),
        in_specs=[pl.BlockSpec((picks // 2, count), lambda g: (g, 0))]
        + [pl.BlockSpec(a.shape, lambda g: (0, 0)) for a in parts],
        out_specs=pl.BlockSpec((picks // 2, depth), lambda g: (g, 0)),
        out_shape=jax.ShapeDtypeStruct((picks, depth), jnp.bfloat16),
        compiler_params=pltpu.CompilerParams(vmem_limit_bytes=56 * 2**20),
        cost_estimate=pl.CostEstimate(flops=10**9, bytes_accessed=4_000_000, transcendentals=0),
    )(hot, *parts)


def base_kernel(tokens, weights, out):
    product = jnp.dot(tokens[...], weights[0], preferred_element_type=jnp.float32)
    out[:, 0, 0] = product.reshape(out.shape[0], out.shape[3], out.shape[4])


def base_products(tokens, weights, planes):
    count, depth = tokens.shape
    columns, _, width = weights.shape
    return pl.pallas_call(
        base_kernel,
        grid=(columns,),
        in_specs=[
            pl.BlockSpec((count, depth), lambda x: (0, 0)),
            pl.BlockSpec((1, depth, width), lambda x: (x, 0, 0)),
        ],
        out_specs=pl.BlockSpec((planes, 1, 1, count // planes, width), lambda x: (0, x // 2, x % 2, 0, 0)),
        out_shape=jax.ShapeDtypeStruct((planes, 2, columns // 2, count // planes, width), jnp.float32),
        compiler_params=pltpu.CompilerParams(vmem_limit_bytes=24 * 2**20),
        cost_estimate=pl.CostEstimate(flops=2 * 10**9, bytes_accessed=8_000_000, transcendentals=0),
    )(tokens, weights)


def place_kernel(core, lists, rows, *refs):
    *before, out = refs
    planes, count, width = out.shape
    at = lax.broadcasted_iota(jnp.int32, (planes * count, 1), 0) + pl.program_id(0) * planes * count
    token = (at // count * 2 + core[0]) * count + at % count
    hot = as_bf16(lists[...] == token)
    placed = jnp.dot(hot, rows[...], preferred_element_type=jnp.float32).reshape(out.shape)
    if before:
        placed = placed + before[0][...]
    out[...] = placed.astype(out.dtype)


def place_rows(core, lists, rows, planes, count, *before):
    width = rows.shape[1]
    block = pl.BlockSpec((2, count, width), lambda z, *_: (z, 0, 0))
    return pl.pallas_call(
        place_kernel,
        grid_spec=pltpu.PrefetchScalarGridSpec(
            num_scalar_prefetch=1,
            grid=(planes // 2,),
            in_specs=[
                pl.BlockSpec((1, lists.shape[1]), lambda z, *_: (0, 0)),
                pl.BlockSpec(rows.shape, lambda z, *_: (0, 0)),
            ]
            + [block] * len(before),
            out_specs=block,
        ),
        out_shape=jax.ShapeDtypeStruct((planes, count, width), jnp.bfloat16),
        compiler_params=pltpu.CompilerParams(vmem_limit_bytes=24 * 2**20),
        cost_estimate=pl.CostEstimate(flops=10**9, bytes_accessed=4_000_000, transcendentals=0),
    )(core, lists, rows, *before)


def plane_sum(values):
    parts = lax.all_to_all(values, "z", split_axis=0, concat_axis=0, tiled=True)
    return jnp.sum(parts.astype(jnp.float32), axis=0)


def per_device(hidden, down_weight, delta_blocks, block_rows, block_cols, tenant_ids, tenant_lists):
    core, column, line = lax.axis_index("core"), lax.axis_index("x"), lax.axis_index("y")
    seq_index = lax.axis_index(SEQ)
    plane = lax.axis_index("z")
    seq_count, lines, columns, planes = (lax.axis_size(a) for a in (SEQ, "y", "x", "z"))
    variants, capacity = tenant_lists.shape
    half = capacity // 2
    own_tokens = hidden.shape[0]
    ff_local, width = down_weight.shape
    slots = delta_blocks.shape[1]
    core_ref = core.reshape(1).astype(jnp.int32)

    gathered = lax.all_gather(hidden, "y", axis=0, tiled=True)
    copies = jnp.broadcast_to(down_weight[None], (columns, ff_local, width))
    weights = lax.all_to_all(copies, "x", split_axis=0, concat_axis=0, tiled=True)

    own_blocks = delta_blocks[0].reshape(slots, BLK // 2, 2 * BLK)
    other_blocks = lax.ppermute(own_blocks, "core", CORE_SWAP)
    rows = lax.dynamic_index_in_dim(block_rows, seq_index, 0, False)
    rows = lax.dynamic_slice_in_dim(rows, plane * 2, 2, 0)
    cols = lax.dynamic_index_in_dim(block_cols, seq_index, 0, False)
    cols = lax.dynamic_slice_in_dim(cols, plane * 2, 2, 0)
    lists = lax.dynamic_index_in_dim(tenant_lists.reshape(lines, columns * capacity), line, 0, False)
    token = jnp.arange(lines * own_tokens, dtype=jnp.int32)
    token = ((token // own_tokens) * columns + column) * own_tokens + token % own_tokens
    spread, hot = spread_blocks(
        core_ref, own_blocks, other_blocks, lists[:, None], token[None, :], seq_count
    )

    picked = pick_rows(hot, (gathered,))
    sent = lax.all_to_all(picked.reshape(columns * 2, half, ff_local), CHIPS, split_axis=0, concat_axis=0, tiled=True)
    delta = delta_products(rows, cols, [sent], spread, seq_count, width)
    received = lax.all_to_all(delta, SEQ, split_axis=0, concat_axis=0, tiled=True)

    base = base_products(gathered, weights, planes)
    base = lax.psum_scatter(
        base.reshape(planes * 2, columns // 2 * own_tokens, width), TENSOR, scatter_dimension=0, tiled=True
    )
    base = base.reshape(columns // 2, own_tokens, width)
    odd = column % 2
    blocks = []
    for flip in range(2):
        pairs = []
        for x in range(columns):
            for c in range(2):
                pairs.append((x * 2 + c, (2 * c + (x % 2 ^ flip)) * 2 + x // 2))
        mine = lax.dynamic_index_in_dim(base, odd ^ flip, 0, False)
        blocks.append(lax.ppermute(mine, CHIPS, pairs))
    base = jnp.where(odd == 0, jnp.concatenate(blocks, 0), jnp.concatenate(blocks[::-1], 0))

    lists = tenant_lists.reshape(variants, 2, half)
    received = received.reshape(variants * half, width)
    swapped = lax.ppermute(received, "core", CORE_SWAP)
    placed = ()
    for side, moved in ((core, received), (1 - core, swapped)):
        held = lax.dynamic_index_in_dim(lists, side, 1, False).reshape(1, variants * half)
        placed = (place_rows(core_ref, held, moved, planes, base.shape[0], *placed),)
    return (plane_sum(placed[0]) + base).astype(jnp.bfloat16)


def solution(mesh):
    fine = Mesh(mesh.devices.reshape(8, 4, 8, 2), ("y", "x", "z", "core"))
    return jax.shard_map(
        per_device,
        mesh=fine,
        in_specs=(
            P(SEQ, TENSOR),
            P(TENSOR, SEQ),
            P(SEQ, TENSOR, None),
            P(),
            P(),
            P(),
            P(),
        ),
        out_specs=P(TENSOR, SEQ),
        check_vma=False,
    )
```

```python
import jax
import jax.numpy as jnp
from jax import lax
from jax.experimental import pallas as pl
from jax.experimental.pallas import tpu as pltpu
from jax.sharding import Mesh, PartitionSpec as P

BLK = 64
LANES = 128
SEQ = ("y", "x")
TENSOR = ("z", "core")
CHIPS = ("x", "core")
CORE_SWAP = [(0, 1), (1, 0)]
STEP_GROUPS = 4
SPREAD_GROUPS = 4


def as_bf16(mask):
    return mask.astype(jnp.float32).astype(jnp.bfloat16)


def spread_kernel(core, own, other, lists, tokens, out, hot):
    low = lax.broadcasted_iota(jnp.int32, (1, LANES), 1) < BLK
    low_f, high_f = as_bf16(low), as_bf16(~low)
    hot[...] = as_bf16(lists[...] == tokens[...])

    def spread(blocks):
        for n in range(blocks.shape[0]):
            block = blocks[n]
            turned = pltpu.roll(block.astype(jnp.float32), BLK, 1).astype(jnp.bfloat16)
            out[0, n, : BLK // 2] = block * low_f + turned * high_f
            out[0, n, BLK // 2 :] = turned * low_f + block * high_f

    pl.when(pl.program_id(0) == 0)(lambda: spread(own))
    pl.when(pl.program_id(0) == 1)(lambda: spread(other))


def spread_blocks(core, own, other, lists, tokens, groups):
    slots, half_rows, lanes = own.shape
    steps = groups // SPREAD_GROUPS
    count = slots // steps
    picks = lists.shape[0]
    return pl.pallas_call(
        spread_kernel,
        grid_spec=pltpu.PrefetchScalarGridSpec(
            num_scalar_prefetch=1,
            grid=(2, steps),
            in_specs=[
                pl.BlockSpec((count, half_rows, lanes), lambda s, g, *_: (g * (1 - s) + (steps - 1) * s, 0, 0)),
                pl.BlockSpec((count, half_rows, lanes), lambda s, g, *_: (g * s, 0, 0)),
                pl.BlockSpec((picks // steps, 1), lambda s, g, *_: (g, 0)),
                pl.BlockSpec(tokens.shape, lambda s, g, *_: (0, 0)),
            ],
            out_specs=[
                pl.BlockSpec((1, count, BLK, LANES), lambda s, g, core: (s ^ core[0], g, 0, 0)),
                pl.BlockSpec((picks // steps, tokens.shape[1]), lambda s, g, *_: (g, 0)),
            ],
        ),
        out_shape=[
            jax.ShapeDtypeStruct((2, slots, BLK, LANES), jnp.bfloat16),
            jax.ShapeDtypeStruct((picks, tokens.shape[1]), jnp.bfloat16),
        ],
        compiler_params=pltpu.CompilerParams(vmem_limit_bytes=56 * 2**20),
        cost_estimate=pl.CostEstimate(flops=0, bytes_accessed=40_000_000, transcendentals=0),
    )(core, own, other, lists, tokens)


def delta_kernel(rows, cols, *refs):
    *sent, stored, out, table, weights, arrived = refs
    step, steps = pl.program_id(0), arrived.shape[0]
    count = stored.shape[1] // steps
    per_group = count // STEP_GROUPS

    def fetch(at):
        slots = pl.ds(pl.multiple_of(at * count, count), count)
        return pltpu.make_async_copy(stored.at[:, slots], weights.at[:, slots], arrived.at[at])

    @pl.when(step == 0)
    def _():
        lax.fori_loop(0, steps, lambda at, _: fetch(at).start(), None)

    tiles = sum(ref.shape[2] for ref in sent) // LANES
    lane_col = lax.broadcasted_iota(jnp.int32, (1, LANES), 1) // BLK
    low_f, high_f = as_bf16(lane_col == 0), as_bf16(lane_col == 1)

    @pl.when(step == 0)
    def _():
        source = lax.broadcasted_iota(jnp.int32, (LANES, 2 * LANES), 0)
        place = lax.broadcasted_iota(jnp.int32, (LANES, 2 * LANES), 1)
        copy, lane = place // LANES, place % LANES
        half = (lane // BLK) ^ copy
        inner = lane % BLK
        wanted = half * BLK + (inner % (BLK // 2)) * 2 + inner // (BLK // 2)
        order = as_bf16(source == wanted)
        for side in range(2):
            tile = 0
            for ref in sent:
                for at in range(0, ref.shape[2], LANES):
                    mine = ref[side, :, at : at + LANES]
                    for x in range(1, ref.shape[0] // 2):
                        mine = mine + ref[2 * x + side, :, at : at + LANES]
                    both = jnp.dot(mine, order, preferred_element_type=jnp.float32).astype(jnp.bfloat16)
                    table[(side * 2) * tiles + tile] = both[:, :LANES]
                    table[(side * 2 + 1) * tiles + tile] = both[:, LANES:]
                    tile += 1

    fetch(step).wait()
    for inner in range(STEP_GROUPS):
        total = None
        for side in range(2):
            pieces, spread = [], []
            for pair in range(per_group // 2):
                picked = []
                for position in range(2):
                    n = inner * per_group + pair * 2 + position
                    slot = step * STEP_GROUPS * per_group + n
                    row = jnp.maximum(rows[side, slot], 0)
                    swapped = (row & 1) ^ position
                    picked.append(table[(side * 2 + swapped) * tiles + row // 2])
                    column = cols[side, slot]
                    column = jnp.where(column >= 0, column & 3, -1)
                    block = weights[side, step * count + n]
                    spread.append(
                        jnp.concatenate(
                            [block * as_bf16(lane_col == column), block * as_bf16(lane_col + 2 == column)], axis=1
                        )
                    )
                pieces.append(picked[0] * low_f + picked[1] * high_f)
            product = jnp.dot(
                jnp.concatenate(pieces, axis=1), jnp.concatenate(spread, axis=0), preferred_element_type=jnp.float32
            )
            total = product if total is None else total + product
        out[inner] = total.astype(out.dtype)


def delta_products(rows, cols, sent, weights, groups, width):
    count = sent[0].shape[1]
    tiles = sum(a.shape[2] for a in sent) // LANES
    return pl.pallas_call(
        delta_kernel,
        grid_spec=pltpu.PrefetchScalarGridSpec(
            num_scalar_prefetch=2,
            grid=(groups // STEP_GROUPS,),
            in_specs=[pl.BlockSpec(a.shape, lambda g, *_: (0, 0, 0)) for a in sent]
            + [pl.BlockSpec(memory_space=pl.ANY)],
            out_specs=pl.BlockSpec((STEP_GROUPS, count, width), lambda g, *_: (g, 0, 0)),
            scratch_shapes=[
                pltpu.VMEM((4 * tiles, count, LANES), jnp.bfloat16),
                pltpu.VMEM(weights.shape, jnp.bfloat16),
                pltpu.SemaphoreType.DMA((groups // STEP_GROUPS,)),
            ],
        ),
        out_shape=jax.ShapeDtypeStruct((groups, count, width), jnp.bfloat16),
        compiler_params=pltpu.CompilerParams(vmem_limit_bytes=48 * 2**20),
        cost_estimate=pl.CostEstimate(flops=2 * 10**9, bytes_accessed=20_000_000, transcendentals=0),
    )(rows, cols, *sent, weights)


def pick_kernel(hot, part, *refs):
    refs[-1][...] = jnp.dot(hot[...], part[...], preferred_element_type=jnp.float32).astype(jnp.bfloat16)


def pick_rows(hot, part, width, *earlier):
    picks, count = hot.shape
    depth = part.shape[1]
    return pl.pallas_call(
        pick_kernel,
        grid=(depth // width,),
        in_specs=[pl.BlockSpec((picks, count), lambda g: (0, 0)), pl.BlockSpec((count, width), lambda g: (0, g))]
        + [pl.BlockSpec(memory_space=pl.ANY)] * len(earlier),
        out_specs=pl.BlockSpec((picks, width), lambda g: (0, g)),
        out_shape=jax.ShapeDtypeStruct((picks, depth), jnp.bfloat16),
        compiler_params=pltpu.CompilerParams(vmem_limit_bytes=56 * 2**20),
        cost_estimate=pl.CostEstimate(flops=10**9, bytes_accessed=4_000_000, transcendentals=0),
    )(hot, part, *earlier)


def base_kernel(tokens, weights, out):
    product = jnp.dot(tokens[...], weights[0], preferred_element_type=jnp.float32)
    out[:, 0, 0] = product.reshape(out.shape[0], out.shape[3], out.shape[4])


def base_products(tokens, weights, planes):
    count, depth = tokens.shape
    columns, _, width = weights.shape
    return pl.pallas_call(
        base_kernel,
        grid=(columns,),
        in_specs=[
            pl.BlockSpec((count, depth), lambda x: (0, 0)),
            pl.BlockSpec((1, depth, width), lambda x: (x, 0, 0)),
        ],
        out_specs=pl.BlockSpec((planes, 1, 1, count // planes, width), lambda x: (0, x // 2, x % 2, 0, 0)),
        out_shape=jax.ShapeDtypeStruct((planes, 2, columns // 2, count // planes, width), jnp.float32),
        compiler_params=pltpu.CompilerParams(vmem_limit_bytes=24 * 2**20),
        cost_estimate=pl.CostEstimate(flops=2 * 10**9, bytes_accessed=8_000_000, transcendentals=0),
    )(tokens, weights)


def place_kernel(core, lists, rows, *refs):
    *before, out = refs
    planes, count, width = out.shape
    at = lax.broadcasted_iota(jnp.int32, (planes * count, 1), 0) + pl.program_id(0) * planes * count
    token = (at // count * 2 + core[0]) * count + at % count
    hot = as_bf16(lists[...] == token)
    placed = jnp.dot(hot, rows[...], preferred_element_type=jnp.float32).reshape(out.shape)
    if before:
        placed = placed + before[0][...]
    out[...] = placed.astype(out.dtype)


def place_rows(core, lists, rows, planes, count, *before):
    width = rows.shape[1]
    block = pl.BlockSpec((2, count, width), lambda z, *_: (z, 0, 0))
    return pl.pallas_call(
        place_kernel,
        grid_spec=pltpu.PrefetchScalarGridSpec(
            num_scalar_prefetch=1,
            grid=(planes // 2,),
            in_specs=[
                pl.BlockSpec((1, lists.shape[1]), lambda z, *_: (0, 0)),
                pl.BlockSpec(rows.shape, lambda z, *_: (0, 0)),
            ]
            + [block] * len(before),
            out_specs=block,
        ),
        out_shape=jax.ShapeDtypeStruct((planes, count, width), jnp.bfloat16),
        compiler_params=pltpu.CompilerParams(vmem_limit_bytes=24 * 2**20),
        cost_estimate=pl.CostEstimate(flops=10**9, bytes_accessed=4_000_000, transcendentals=0),
    )(core, lists, rows, *before)


def plane_sum(values):
    parts = lax.all_to_all(values, "z", split_axis=0, concat_axis=0, tiled=True)
    return jnp.sum(parts.astype(jnp.float32), axis=0)


def per_device(hidden, down_weight, delta_blocks, block_rows, block_cols, tenant_ids, tenant_lists):
    core, column, line = lax.axis_index("core"), lax.axis_index("x"), lax.axis_index("y")
    seq_index = lax.axis_index(SEQ)
    plane = lax.axis_index("z")
    seq_count, lines, columns, planes = (lax.axis_size(a) for a in (SEQ, "y", "x", "z"))
    variants, capacity = tenant_lists.shape
    half = capacity // 2
    own_tokens = hidden.shape[0]
    ff_local, width = down_weight.shape
    slots = delta_blocks.shape[1]
    core_ref = core.reshape(1).astype(jnp.int32)

    gathered = lax.all_gather(hidden, "y", axis=0, tiled=True)
    copies = jnp.broadcast_to(down_weight[None], (columns, ff_local, width))
    weights = lax.all_to_all(copies, "x", split_axis=0, concat_axis=0, tiled=True)

    own_blocks = delta_blocks[0].reshape(slots, BLK // 2, 2 * BLK)
    other_blocks = lax.ppermute(own_blocks, "core", CORE_SWAP)
    rows = lax.dynamic_index_in_dim(block_rows, seq_index, 0, False)
    rows = lax.dynamic_slice_in_dim(rows, plane * 2, 2, 0)
    cols = lax.dynamic_index_in_dim(block_cols, seq_index, 0, False)
    cols = lax.dynamic_slice_in_dim(cols, plane * 2, 2, 0)
    lists = lax.dynamic_index_in_dim(tenant_lists.reshape(lines, columns * capacity), line, 0, False)
    token = jnp.arange(lines * own_tokens, dtype=jnp.int32)
    token = ((token // own_tokens) * columns + column) * own_tokens + token % own_tokens
    spread, hot = spread_blocks(
        core_ref, own_blocks, other_blocks, lists[:, None], token[None, :], seq_count
    )

    picked = pick_rows(hot, gathered, 2 * LANES)
    sent = lax.all_to_all(picked.reshape(columns * 2, half, ff_local), CHIPS, split_axis=0, concat_axis=0, tiled=True)
    delta = delta_products(rows, cols, [sent], spread, seq_count, width)
    received = lax.all_to_all(delta, SEQ, split_axis=0, concat_axis=0, tiled=True)

    base = base_products(gathered, weights, planes)
    base = lax.psum_scatter(
        base.reshape(planes * 2, columns // 2 * own_tokens, width), TENSOR, scatter_dimension=0, tiled=True
    )
    base = base.reshape(columns // 2, own_tokens, width)
    odd = column % 2
    blocks = []
    for flip in range(2):
        pairs = []
        for x in range(columns):
            for c in range(2):
                pairs.append((x * 2 + c, (2 * c + (x % 2 ^ flip)) * 2 + x // 2))
        mine = lax.dynamic_index_in_dim(base, odd ^ flip, 0, False)
        blocks.append(lax.ppermute(mine, CHIPS, pairs))
    base = jnp.where(odd == 0, jnp.concatenate(blocks, 0), jnp.concatenate(blocks[::-1], 0))

    lists = tenant_lists.reshape(variants, 2, half)
    received = received.reshape(variants * half, width)
    swapped = lax.ppermute(received, "core", CORE_SWAP)
    placed = ()
    for side, moved in ((core, received), (1 - core, swapped)):
        held = lax.dynamic_index_in_dim(lists, side, 1, False).reshape(1, variants * half)
        placed = (place_rows(core_ref, held, moved, planes, base.shape[0], *placed),)
    return (plane_sum(placed[0]) + base).astype(jnp.bfloat16)


def solution(mesh):
    fine = Mesh(mesh.devices.reshape(8, 4, 8, 2), ("y", "x", "z", "core"))
    return jax.shard_map(
        per_device,
        mesh=fine,
        in_specs=(
            P(SEQ, TENSOR),
            P(TENSOR, SEQ),
            P(SEQ, TENSOR, None),
            P(),
            P(),
            P(),
            P(),
        ),
        out_specs=P(TENSOR, SEQ),
        check_vma=False,
    )
```

```python
import jax
import jax.numpy as jnp
from jax import lax
from jax.experimental import pallas as pl
from jax.experimental.pallas import tpu as pltpu
from jax.sharding import Mesh, PartitionSpec as P

BLK = 64
LANES = 128
SEQ = ("y", "x")
TENSOR = ("z", "core")
CHIPS = ("x", "core")
CORE_SWAP = [(0, 1), (1, 0)]
STEP_GROUPS = 4
SPREAD_GROUPS = 4


def as_bf16(mask):
    return mask.astype(jnp.float32).astype(jnp.bfloat16)


def spread_kernel(core, own, other, lists, tokens, out, hot):
    low = lax.broadcasted_iota(jnp.int32, (1, LANES), 1) < BLK
    low_f, high_f = as_bf16(low), as_bf16(~low)
    hot[...] = as_bf16(lists[...] == tokens[...])

    def spread(blocks):
        for n in range(blocks.shape[0]):
            block = blocks[n]
            turned = pltpu.roll(block.astype(jnp.float32), BLK, 1).astype(jnp.bfloat16)
            out[0, n, : BLK // 2] = block * low_f + turned * high_f
            out[0, n, BLK // 2 :] = turned * low_f + block * high_f

    pl.when(pl.program_id(0) == 0)(lambda: spread(own))
    pl.when(pl.program_id(0) == 1)(lambda: spread(other))


def spread_blocks(core, own, other, lists, tokens, groups):
    slots, half_rows, lanes = own.shape
    steps = groups // SPREAD_GROUPS
    count = slots // steps
    picks = lists.shape[0]
    return pl.pallas_call(
        spread_kernel,
        grid_spec=pltpu.PrefetchScalarGridSpec(
            num_scalar_prefetch=1,
            grid=(2, steps),
            in_specs=[
                pl.BlockSpec((count, half_rows, lanes), lambda s, g, *_: (g * (1 - s) + (steps - 1) * s, 0, 0)),
                pl.BlockSpec((count, half_rows, lanes), lambda s, g, *_: (g * s, 0, 0)),
                pl.BlockSpec((picks // steps, 1), lambda s, g, *_: (g, 0)),
                pl.BlockSpec(tokens.shape, lambda s, g, *_: (0, 0)),
            ],
            out_specs=[
                pl.BlockSpec((1, count, BLK, LANES), lambda s, g, core: (s ^ core[0], g, 0, 0)),
                pl.BlockSpec((picks // steps, tokens.shape[1]), lambda s, g, *_: (g, 0)),
            ],
        ),
        out_shape=[
            jax.ShapeDtypeStruct((2, slots, BLK, LANES), jnp.bfloat16),
            jax.ShapeDtypeStruct((picks, tokens.shape[1]), jnp.bfloat16),
        ],
        compiler_params=pltpu.CompilerParams(vmem_limit_bytes=56 * 2**20),
        cost_estimate=pl.CostEstimate(flops=0, bytes_accessed=40_000_000, transcendentals=0),
    )(core, own, other, lists, tokens)


def delta_kernel(rows, cols, *refs):
    *sent, stored, out, table, weights, arrived = refs
    step, steps = pl.program_id(0), arrived.shape[0]
    count = stored.shape[1] // steps
    per_group = count // STEP_GROUPS

    def fetch(at):
        slots = pl.ds(pl.multiple_of(at * count, count), count)
        return pltpu.make_async_copy(stored.at[:, slots], weights.at[:, slots], arrived.at[at])

    @pl.when(step == 0)
    def _():
        lax.fori_loop(0, steps, lambda at, _: fetch(at).start(), None)

    tiles = sum(ref.shape[2] for ref in sent) // LANES
    lane_col = lax.broadcasted_iota(jnp.int32, (1, LANES), 1) // BLK
    low_f, high_f = as_bf16(lane_col == 0), as_bf16(lane_col == 1)

    @pl.when(step == 0)
    def _():
        source = lax.broadcasted_iota(jnp.int32, (LANES, 2 * LANES), 0)
        place = lax.broadcasted_iota(jnp.int32, (LANES, 2 * LANES), 1)
        copy, lane = place // LANES, place % LANES
        half = (lane // BLK) ^ copy
        inner = lane % BLK
        wanted = half * BLK + (inner % (BLK // 2)) * 2 + inner // (BLK // 2)
        order = as_bf16(source == wanted)
        for side in range(2):
            tile = 0
            for ref in sent:
                for at in range(0, ref.shape[2], LANES):
                    mine = ref[side, :, at : at + LANES]
                    for x in range(1, ref.shape[0] // 2):
                        mine = mine + ref[2 * x + side, :, at : at + LANES]
                    both = jnp.dot(mine, order, preferred_element_type=jnp.float32).astype(jnp.bfloat16)
                    table[(side * 2) * tiles + tile] = both[:, :LANES]
                    table[(side * 2 + 1) * tiles + tile] = both[:, LANES:]
                    tile += 1

    fetch(step).wait()
    for inner in range(STEP_GROUPS):
        total = None
        for side in range(2):
            pieces, spread = [], []
            for pair in range(per_group // 2):
                picked = []
                for position in range(2):
                    n = inner * per_group + pair * 2 + position
                    slot = step * STEP_GROUPS * per_group + n
                    row = jnp.maximum(rows[side, slot], 0)
                    swapped = (row & 1) ^ position
                    picked.append(table[(side * 2 + swapped) * tiles + row // 2])
                    column = cols[side, slot]
                    column = jnp.where(column >= 0, column & 3, -1)
                    block = weights[side, step * count + n]
                    spread.append(
                        jnp.concatenate(
                            [block * as_bf16(lane_col == column), block * as_bf16(lane_col + 2 == column)], axis=1
                        )
                    )
                pieces.append(picked[0] * low_f + picked[1] * high_f)
            product = jnp.dot(
                jnp.concatenate(pieces, axis=1), jnp.concatenate(spread, axis=0), preferred_element_type=jnp.float32
            )
            total = product if total is None else total + product
        out[inner] = total.astype(out.dtype)


def delta_products(rows, cols, sent, weights, groups, width):
    count = sent[0].shape[1]
    tiles = sum(a.shape[2] for a in sent) // LANES
    return pl.pallas_call(
        delta_kernel,
        grid_spec=pltpu.PrefetchScalarGridSpec(
            num_scalar_prefetch=2,
            grid=(groups // STEP_GROUPS,),
            in_specs=[pl.BlockSpec(a.shape, lambda g, *_: (0, 0, 0)) for a in sent]
            + [pl.BlockSpec(memory_space=pl.ANY)],
            out_specs=pl.BlockSpec((STEP_GROUPS, count, width), lambda g, *_: (g, 0, 0)),
            scratch_shapes=[
                pltpu.VMEM((4 * tiles, count, LANES), jnp.bfloat16),
                pltpu.VMEM(weights.shape, jnp.bfloat16),
                pltpu.SemaphoreType.DMA((groups // STEP_GROUPS,)),
            ],
        ),
        out_shape=jax.ShapeDtypeStruct((groups, count, width), jnp.bfloat16),
        compiler_params=pltpu.CompilerParams(vmem_limit_bytes=48 * 2**20),
        cost_estimate=pl.CostEstimate(flops=2 * 10**9, bytes_accessed=20_000_000, transcendentals=0),
    )(rows, cols, *sent, weights)


def pick_kernel(hot, part, *refs):
    refs[-1][...] = jnp.dot(hot[...], part[...], preferred_element_type=jnp.float32).astype(jnp.bfloat16)


def pick_rows(hot, part, width, *earlier):
    picks, count = hot.shape
    depth = part.shape[1]
    return pl.pallas_call(
        pick_kernel,
        grid=(depth // width,),
        in_specs=[pl.BlockSpec((picks, count), lambda g: (0, 0)), pl.BlockSpec((count, width), lambda g: (0, g))]
        + [pl.BlockSpec(memory_space=pl.ANY)] * len(earlier),
        out_specs=pl.BlockSpec((picks, width), lambda g: (0, g)),
        out_shape=jax.ShapeDtypeStruct((picks, depth), jnp.bfloat16),
        compiler_params=pltpu.CompilerParams(vmem_limit_bytes=56 * 2**20),
        cost_estimate=pl.CostEstimate(flops=10**9, bytes_accessed=4_000_000, transcendentals=0),
    )(hot, part, *earlier)


def base_kernel(tokens, weights, out):
    product = jnp.dot(tokens[...], weights[0], preferred_element_type=jnp.float32)
    out[:, 0, 0] = product.reshape(out.shape[0], out.shape[3], out.shape[4])


def base_products(tokens, weights, planes):
    count, depth = tokens.shape
    columns, _, width = weights.shape
    return pl.pallas_call(
        base_kernel,
        grid=(columns,),
        in_specs=[
            pl.BlockSpec((count, depth), lambda x: (0, 0)),
            pl.BlockSpec((1, depth, width), lambda x: (x, 0, 0)),
        ],
        out_specs=pl.BlockSpec((planes, 1, 1, count // planes, width), lambda x: (0, x // 2, x % 2, 0, 0)),
        out_shape=jax.ShapeDtypeStruct((planes, 2, columns // 2, count // planes, width), jnp.float32),
        compiler_params=pltpu.CompilerParams(vmem_limit_bytes=24 * 2**20),
        cost_estimate=pl.CostEstimate(flops=2 * 10**9, bytes_accessed=8_000_000, transcendentals=0),
    )(tokens, weights)


def place_kernel(core, lists, rows, *refs):
    *before, out = refs
    planes, count, width = out.shape
    at = lax.broadcasted_iota(jnp.int32, (planes * count, 1), 0) + pl.program_id(0) * planes * count
    token = (at // count * 2 + core[0]) * count + at % count
    hot = as_bf16(lists[...] == token)
    placed = jnp.dot(hot, rows[...], preferred_element_type=jnp.float32).reshape(out.shape)
    if before:
        placed = placed + before[0][...]
    out[...] = placed.astype(out.dtype)


def place_rows(core, lists, rows, planes, count, *before):
    width = rows.shape[1]
    block = pl.BlockSpec((2, count, width), lambda z, *_: (z, 0, 0))
    return pl.pallas_call(
        place_kernel,
        grid_spec=pltpu.PrefetchScalarGridSpec(
            num_scalar_prefetch=1,
            grid=(planes // 2,),
            in_specs=[
                pl.BlockSpec((1, lists.shape[1]), lambda z, *_: (0, 0)),
                pl.BlockSpec(rows.shape, lambda z, *_: (0, 0)),
            ]
            + [block] * len(before),
            out_specs=block,
        ),
        out_shape=jax.ShapeDtypeStruct((planes, count, width), jnp.bfloat16),
        compiler_params=pltpu.CompilerParams(vmem_limit_bytes=24 * 2**20),
        cost_estimate=pl.CostEstimate(flops=10**9, bytes_accessed=4_000_000, transcendentals=0),
    )(core, lists, rows, *before)


def plane_sum(values):
    parts = lax.all_to_all(values, "z", split_axis=0, concat_axis=0, tiled=True)
    return jnp.sum(parts.astype(jnp.float32), axis=0)


def per_device(hidden, down_weight, delta_blocks, block_rows, block_cols, tenant_ids, tenant_lists):
    core, column, line = lax.axis_index("core"), lax.axis_index("x"), lax.axis_index("y")
    seq_index = lax.axis_index(SEQ)
    plane = lax.axis_index("z")
    seq_count, lines, columns, planes = (lax.axis_size(a) for a in (SEQ, "y", "x", "z"))
    variants, capacity = tenant_lists.shape
    half = capacity // 2
    own_tokens = hidden.shape[0]
    ff_local, width = down_weight.shape
    slots = delta_blocks.shape[1]
    core_ref = core.reshape(1).astype(jnp.int32)

    copies = jnp.broadcast_to(hidden[None], (lines, own_tokens, ff_local))
    gathered = lax.all_to_all(copies, "y", split_axis=0, concat_axis=0, tiled=True)
    gathered = gathered.reshape(lines * own_tokens, ff_local)
    weights = lax.all_gather(down_weight, "x", axis=0, tiled=False)

    own_blocks = delta_blocks[0].reshape(slots, BLK // 2, 2 * BLK)
    other_blocks = lax.ppermute(own_blocks, "core", CORE_SWAP)
    rows = lax.dynamic_index_in_dim(block_rows, seq_index, 0, False)
    rows = lax.dynamic_slice_in_dim(rows, plane * 2, 2, 0)
    cols = lax.dynamic_index_in_dim(block_cols, seq_index, 0, False)
    cols = lax.dynamic_slice_in_dim(cols, plane * 2, 2, 0)
    lists = lax.dynamic_index_in_dim(tenant_lists.reshape(lines, columns * capacity), line, 0, False)
    token = jnp.arange(lines * own_tokens, dtype=jnp.int32)
    token = ((token // own_tokens) * columns + column) * own_tokens + token % own_tokens
    spread, hot = spread_blocks(
        core_ref, own_blocks, other_blocks, lists[:, None], token[None, :], seq_count
    )

    picked = pick_rows(hot, gathered, 2 * LANES)
    sent = lax.all_to_all(picked.reshape(columns * 2, half, ff_local), CHIPS, split_axis=0, concat_axis=0, tiled=True)
    delta = delta_products(rows, cols, [sent], spread, seq_count, width)
    received = lax.all_to_all(delta, SEQ, split_axis=0, concat_axis=0, tiled=True)

    base = base_products(gathered, weights, planes)
    base = lax.psum_scatter(
        base.reshape(planes * 2, columns // 2 * own_tokens, width), TENSOR, scatter_dimension=0, tiled=True
    )
    base = base.reshape(columns // 2, own_tokens, width)
    odd = column % 2
    blocks = []
    for flip in range(2):
        pairs = []
        for x in range(columns):
            for c in range(2):
                pairs.append((x * 2 + c, (2 * c + (x % 2 ^ flip)) * 2 + x // 2))
        mine = lax.dynamic_index_in_dim(base, odd ^ flip, 0, False)
        blocks.append(lax.ppermute(mine, CHIPS, pairs))
    base = jnp.where(odd == 0, jnp.concatenate(blocks, 0), jnp.concatenate(blocks[::-1], 0))

    lists = tenant_lists.reshape(variants, 2, half)
    received = received.reshape(variants * half, width)
    swapped = lax.ppermute(received, "core", CORE_SWAP)
    placed = ()
    for side, moved in ((core, received), (1 - core, swapped)):
        held = lax.dynamic_index_in_dim(lists, side, 1, False).reshape(1, variants * half)
        placed = (place_rows(core_ref, held, moved, planes, base.shape[0], *placed),)
    return (plane_sum(placed[0]) + base).astype(jnp.bfloat16)


def solution(mesh):
    fine = Mesh(mesh.devices.reshape(8, 4, 8, 2), ("y", "x", "z", "core"))
    return jax.shard_map(
        per_device,
        mesh=fine,
        in_specs=(
            P(SEQ, TENSOR),
            P(TENSOR, SEQ),
            P(SEQ, TENSOR, None),
            P(),
            P(),
            P(),
            P(),
        ),
        out_specs=P(TENSOR, SEQ),
        check_vma=False,
    )
```
